32 devices in a mesh: section: 4 (over y, x), tensor: 8 (over z, core).
Axes of the slice: x: 2, y: 2, z: 4, core: 2. Of those that a mesh axis runs over, the one named last changes fastest.
Arguments:
- queries: bfloat16 [4, 512, 8192], P('section', None, 'tensor'), may hold values from -20 to 20
- key_rows: bfloat16 [4, 512, 1024], P('section'), may hold values from -6 to 6
- value_rows: bfloat16 [4, 512, 1024], P('section'), may hold values from -6 to 6
- out_grad: bfloat16 [4, 512, 8192], P('section', None, 'tensor'), may hold values from -24 to 24
- layer_input: bfloat16 [4, 512, 8192], P('section', 'tensor'), may hold values from -64 to 64
- query_weight: bfloat16 [4, 8192, 8192], P('section', None, 'tensor'), may hold values from -0.0625 to 0.0625
- dion_basis: float32 [4, 8192, 256], P('section', 'tensor'), may hold values from -0.0625 to 0.0625
- lengths: int32 [4, 3], P('section'), may hold values from 1 to 256, 512 in all within a row
Outputs:
- upstream: bfloat16 [4, 512, 8192], P('section', 'tensor')
- left_factor: float32 [4, 8192, 256], P('section', 'tensor')
- right_factor: float32 [4, 8192, 256], P('section', 'tensor')
The draws below stay inside these ranges and needn't reach their ends.
Inputs may be any that keep to these rules, and one draw needn't show every extreme that they name: For each section the lengths of the prompt, the chosen and the rejected response, in that order, summing to 512.
All inputs are finite; a program needn't handle non-finite values.
Results may differ from the reference program's by a relative error of at most 0.022.
Values may be sent and summed in bfloat16 or wider, within the bound.
A program may use at most 128 MiB of HBM per device.

```python
import math
import jax
import jax.numpy as jnp
import numpy as np
from jax import lax

D = 8192
HEADS = 64
HD = 128
GROUP = 8
KV_HEADS = 8
TOK = 512
RANK = 256
N_SECTION = 4
N_TENSOR = 8


def paired_draw(key):
    query_key = jax.random.fold_in(key, 101)
    key_key = jax.random.fold_in(key, 202)
    queries = jnp.clip(jax.random.normal(query_key, (N_SECTION, TOK, HEADS * HD), jnp.float32), -6.0, 6.0)
    key_rows = jnp.clip(jax.random.normal(key_key, (N_SECTION, TOK, HEADS // GROUP * HD), jnp.float32), -6.0, 6.0)
    return (queries, key_rows)


def draw_queries(key, part):
    return paired_draw(key)[0].astype(jnp.bfloat16)


def draw_key_rows(key, part):
    return paired_draw(key)[1].astype(jnp.bfloat16)


def draw_layer_input(key, part):
    base_key = jax.random.fold_in(key, 404)
    column_key = jax.random.fold_in(key, 505)
    row_key = jax.random.fold_in(key, 606)
    column_ids = jnp.arange(D, dtype=jnp.float32)
    ramp = jnp.power(10.0, column_ids / (D - 1.0) - 0.5)
    rough = jax.random.uniform(column_key, (N_SECTION, 1, D), jnp.float32, 0.7, 1.3)
    row_scale = jax.random.uniform(row_key, (N_SECTION, TOK, 1), jnp.float32, 0.6, 1.6)
    base = jnp.clip(jax.random.normal(base_key, (N_SECTION, TOK, D), jnp.float32), -6.0, 6.0)
    return (base * ramp[None, None, :] * rough * row_scale).astype(jnp.bfloat16)


def steps_of(rng, dims, split, smallest, top_value):
    factor_of, own = 1.0, jax.random.fold_in(rng, 6)
    for dim, shards_of in split:
        heights = jnp.exp(jax.random.uniform(jax.random.fold_in(own, dim), (shards_of,), jnp.float32, smallest / len(split), top_value / len(split)))
        factor_of = factor_of * jnp.repeat(heights, dims[dim] // shards_of).reshape([-1 if axis == dim else 1 for axis in range(len(dims))])
    return factor_of


def split_up(count, total, reach, slope):
    loads = [(1 << 20) // math.isqrt(standing ** slope) + 1 for standing in range(2, count + 1)]
    spare, counts = total - reach - (count - 1), [1] * (count - 1)
    while spare > 0:
        movable = [i for i in range(count - 1) if counts[i] < reach]
        mass, left = sum([loads[i] for i in movable]), spare
        for i in movable:
            extra = min(reach - counts[i], max(1, left * loads[i] // mass), spare)
            counts[i] = counts[i] + extra
            spare = spare - extra
    return np.array([reach] + counts)


def uneven_parts(own_key, count, total, reach, slope):
    if count == 2:
        one = jax.random.randint(own_key, (), max(1, total - reach), min(reach, total - 1) + 1)
        return jnp.stack([one, total - one])
    sizes = jnp.asarray(split_up(count, total, reach, slope), jnp.int32)
    twos = (count - 1) // 2
    giver, receiver = sizes[1:1 + 2 * twos:2], sizes[2:2 + 2 * twos:2]
    room = jnp.minimum(giver - 1, reach - receiver)
    moved = jax.random.randint(jax.random.fold_in(own_key, 1), (twos,), 0, 1 << 20) % (room + 1)
    sizes = sizes.at[1:1 + 2 * twos:2].set(giver - moved).at[2:2 + 2 * twos:2].set(receiver + moved)
    return sizes[jax.random.permutation(jax.random.fold_in(own_key, 2), count)]


def noise(stream_key, extent, scale, most, pieces=(), kind=jnp.bfloat16):
    array = jax.random.normal(stream_key, extent, jnp.float32) * scale
    if len(pieces) > 0:
        array = steps_of(stream_key, extent, pieces, -0.22, 0.18) * array
    return jnp.clip(array, min=-most, max=most).astype(kind)


def setup_inputs(seed: int = 0) -> dict:
    key_of = jax.random.split(jax.random.key(seed), 9)
    queries = draw_queries(jax.random.fold_in(key_of[8], 71), 0)
    key_rows = draw_key_rows(jax.random.fold_in(key_of[8], 71), 0)
    value_rows = noise(key_of[2], (N_SECTION, TOK, KV_HEADS * HD), 1.0, 6.0, ((0, 4),))
    out_grad = noise(key_of[3], (N_SECTION, TOK, HEADS * HD), 4.0, 24.0, ((0, 4), (2, 8)))
    layer_input = draw_layer_input(jax.random.fold_in(key_of[8], 71), 0)
    query_weight = noise(key_of[5], (N_SECTION, D, HEADS * HD), D ** -0.5, 0.0625, ((0, 4), (2, 8)))
    dion_basis = noise(key_of[6], (N_SECTION, HEADS * HD, RANK), (HEADS * HD) ** -0.5, 0.0625, ((0, 4), (1, 8)), jnp.float32)
    lengths = jax.vmap(lambda own: uneven_parts(own, 3, TOK, TOK // 2, 1))(jax.random.split(key_of[7], N_SECTION)).reshape((N_SECTION, 3)).astype(jnp.int32)
    return dict(queries=queries, key_rows=key_rows, value_rows=value_rows, out_grad=out_grad, layer_input=layer_input, query_weight=query_weight, dion_basis=dion_basis, lengths=lengths)


rope_base = 500000.0
highest = lax.Precision.HIGHEST

def tree_layout(lengths_row, token_count):
    token_ids = jnp.arange(token_count, dtype=jnp.int32)
    bound_one = lengths_row[0]
    bound_two = lengths_row[0] + lengths_row[1]
    positions = jnp.where(token_ids < bound_two, token_ids, token_ids - lengths_row[1]).astype(jnp.float32)
    row_ids = token_ids[:, None]
    col_ids = token_ids[None, :]
    crossed = (row_ids >= bound_two) & (col_ids >= bound_one) & (col_ids < bound_two)
    visible = (col_ids <= row_ids) & jnp.logical_not(crossed)
    return (positions, visible)

def unrotate(rotated, positions):
    head_dim = rotated.shape[-1]
    half_dim = head_dim // 2
    freq_ids = jnp.arange(half_dim, dtype=jnp.float32)
    inverse = jnp.exp(-math.log(rope_base) * 2.0 * freq_ids / head_dim)
    angles = positions[:, None] * inverse[None, :]
    cosine = jnp.cos(angles)[:, None, :]
    sine_part = jnp.sin(angles)[:, None, :]
    first_half = rotated[..., :half_dim]
    second_half = rotated[..., half_dim:]
    return jnp.concatenate([first_half * cosine + second_half * sine_part, second_half * cosine - first_half * sine_part], axis=-1)

def group_backward(query_block, grad_block, key_block, value_block, visible):
    score_scale = 1.0 / math.sqrt(query_block.shape[-1])
    query_wide = query_block.astype(jnp.float32)
    grad_wide = grad_block.astype(jnp.float32)
    key_wide = key_block.astype(jnp.float32)
    value_wide = value_block.astype(jnp.float32)
    scores = jnp.einsum('qhd,kd->hqk', query_wide, key_wide) * score_scale
    scores = jnp.where(visible[None], scores, -jnp.inf)
    row_max = lax.optimization_barrier(jnp.max(scores, axis=-1, keepdims=True))
    exp_scores = jnp.exp(scores - row_max)
    weights = exp_scores / lax.optimization_barrier(jnp.sum(exp_scores, axis=-1, keepdims=True))
    weights_low = weights.astype(jnp.bfloat16)
    outputs = jnp.einsum('hqk,kd->qhd', weights_low.astype(jnp.float32), value_wide)
    out_dot = lax.optimization_barrier(jnp.sum(grad_wide * outputs, axis=-1))
    prob_grad = jnp.einsum('qhd,kd->hqk', grad_wide, value_wide)
    score_grad = (weights * (prob_grad - out_dot.T[:, :, None])).astype(jnp.bfloat16)
    return jnp.einsum('hqk,kd->qhd', score_grad.astype(jnp.float32), key_wide) * score_scale

def section_backward(section_items):
    queries, key_rows, value_rows, out_grad, layer_input, query_weight, dion_basis, lengths = section_items
    token_count = queries.shape[0]
    positions, visible = tree_layout(lengths, token_count)
    query_heads = queries.reshape(token_count, HEADS, HD)
    grad_heads = out_grad.reshape(token_count, HEADS, HD)

    def one_group(group_id):
        query_block = lax.dynamic_slice_in_dim(query_heads, (group_id * GROUP).astype(jnp.int32), GROUP, 1)
        grad_block = lax.dynamic_slice_in_dim(grad_heads, (group_id * GROUP).astype(jnp.int32), GROUP, 1)
        key_block = lax.dynamic_slice_in_dim(key_rows, (group_id * HD).astype(jnp.int32), HD, 1)
        value_block = lax.dynamic_slice_in_dim(value_rows, (group_id * HD).astype(jnp.int32), HD, 1)
        return group_backward(query_block, grad_block, key_block, value_block, visible)
    rotated = lax.map(one_group, jnp.arange(HEADS // GROUP, dtype=jnp.int32))
    rotated = jnp.transpose(rotated, (1, 0, 2, 3)).reshape(token_count, HEADS, HD)
    query_grad = unrotate(rotated, positions).reshape(token_count, HEADS * HD).astype(jnp.bfloat16)
    block_width = HEADS * HD // N_TENSOR

    def add_block(block_id, running):
        block_start = jnp.asarray(block_id * block_width).astype(jnp.int32)
        grad_piece = lax.dynamic_slice_in_dim(query_grad, block_start, block_width, 1)
        weight_piece = lax.dynamic_slice_in_dim(query_weight, block_start, block_width, 1)
        partial_sum = lax.dot_general(grad_piece.astype(jnp.float32), weight_piece.astype(jnp.float32), (((1,), (1,)), ((), ())), preferred_element_type=jnp.float32)
        rounded = lax.optimization_barrier(partial_sum.astype(jnp.bfloat16))
        return running + rounded.astype(jnp.float32)
    layer_grad = lax.fori_loop(0, N_TENSOR, add_block, jnp.zeros((token_count, D), jnp.float32)).astype(jnp.bfloat16)
    grad_wide = query_grad.astype(jnp.float32)
    input_wide = layer_input.astype(jnp.float32)
    projected = jnp.dot(grad_wide, dion_basis, precision=highest)
    left_raw = lax.dot_general(input_wide, projected, (((0,), (0,)), ((), ())), precision=highest)
    gram_total = lax.dot_general(left_raw, left_raw, (((0,), (0,)), ((), ())), precision=highest)
    lower_factor = jnp.linalg.cholesky(gram_total)
    left_orth = lax.linalg.triangular_solve(lower_factor, left_raw, left_side=False, lower=True, transpose_a=True)
    mixed = jnp.dot(input_wide, left_orth, precision=highest)
    right_factor = lax.dot_general(grad_wide, mixed, (((0,), (0,)), ((), ())), precision=highest)
    return (layer_grad, left_orth * math.sqrt(D), right_factor)

def reference(queries, key_rows, value_rows, out_grad, layer_input, query_weight, dion_basis, lengths):
    layer_grad, left_factor, right_factor = lax.map(section_backward, (queries, key_rows, value_rows, out_grad, layer_input, query_weight, dion_basis, lengths))
    upstream = jnp.concatenate([layer_grad[1:], jnp.zeros_like(layer_grad[:1])], axis=0)
    return (upstream, left_factor, right_factor)
```

```python
import functools
import math

import jax
import jax.numpy as jnp
from jax import lax
from jax.experimental import pallas as pl
from jax.experimental.pallas import tpu as pltpu
from jax.sharding import PartitionSpec as P

D = 8192
HD = 128
GROUP = 8
MESH = pl.DeviceIdType.MESH

rope_base = 500000.0
highest = lax.Precision.HIGHEST
f32 = jnp.float32
bf16 = jnp.bfloat16


def shifted(value, axis, steps):
    count = lax.axis_size(axis)
    first, last = (max(0, -steps), min(count, count - steps))
    return lax.ppermute(value, axis, [(source, source + steps) for source in range(first, last)])


def tree_layout(lengths_row, token_count):
    token_ids = jnp.arange(token_count, dtype=jnp.int32)
    bound_one = lengths_row[0]
    bound_two = lengths_row[0] + lengths_row[1]
    positions = jnp.where(token_ids < bound_two, token_ids, token_ids - lengths_row[1]).astype(f32)
    row_ids = token_ids[:, None]
    col_ids = token_ids[None, :]
    crossed = (row_ids >= bound_two) & (col_ids >= bound_one) & (col_ids < bound_two)
    visible = (col_ids <= row_ids) & jnp.logical_not(crossed)
    bias = jnp.where(visible, 0.0, -1e30).astype(f32)
    freq_ids = jnp.arange(HD // 2, dtype=f32)
    inverse = jnp.exp(-math.log(rope_base) * 2.0 * freq_ids / HD)
    angles = positions[:, None] * inverse[None, :]
    scale = 1.0 / math.sqrt(HD)
    cosine, sine = jnp.cos(angles) * scale, jnp.sin(angles) * scale
    return (
        bias,
        jnp.concatenate([cosine, cosine], axis=-1),
        jnp.concatenate([sine, -sine], axis=-1),
    )


def nt(a, b):
    return lax.dot_general(a, b, (((1,), (1,)), ((), ())), preferred_element_type=f32)


def attend(q_ref, g_ref, k_ref, v_ref, bias_ref, cos_ref, sin_ref, out_ref):
    tokens, width = q_ref.shape
    half = tokens // 2
    scale = 1.0 / math.sqrt(HD)

    def head(h, carry):
        lanes = pl.ds(pl.multiple_of(h * HD, HD), HD)
        for part in range(2):
            rows, seen = pl.ds(part * half, half), pl.ds(0, (part + 1) * half)
            keys, values = k_ref[seen, :], v_ref[seen, :]
            q, g = q_ref[rows, lanes], g_ref[rows, lanes]
            scores = nt(q, keys) * scale + bias_ref[rows, seen]
            exps = jnp.exp(scores - jnp.max(scores, axis=-1, keepdims=True))
            weights = exps * (1.0 / jnp.sum(exps, axis=-1, keepdims=True))
            outputs = jnp.dot(weights.astype(bf16), values, preferred_element_type=f32)
            out_dot = jnp.sum(g.astype(f32) * outputs, axis=-1, keepdims=True)
            score_grad = (weights * (nt(g, values) - out_dot)).astype(bf16)
            rotated = jnp.dot(score_grad, keys, preferred_element_type=f32)
            swapped = jnp.concatenate([rotated[:, HD // 2 :], rotated[:, : HD // 2]], axis=-1)
            out_ref[rows, lanes] = (
                rotated * cos_ref[rows, :] + swapped * sin_ref[rows, :]
            ).astype(bf16)
        return carry

    lax.fori_loop(0, width // HD, head, 0)


def attention_kernel(
    n, q_ref, g_ref, k_ref, v_ref, bias_ref, cos_ref, sin_ref, x_ref, out_ref, cols_ref,
    send_sem, recv_sem,
):
    me = lax.axis_index("tensor")
    rows = x_ref.shape[0]
    width = x_ref.shape[1] // n
    barrier = pltpu.get_barrier_semaphore()
    for step in range(1, n):
        pl.semaphore_signal(
            barrier, inc=1, device_id={"tensor": lax.rem(me + step, n)}, device_id_type=MESH
        )
    pl.semaphore_wait(barrier, n - 1)
    mine = pl.ds(pl.multiple_of(me * rows, rows), rows)
    copies = []
    for step in range(1, n):
        peer = lax.rem(me + step, n)
        copies.append(
            pltpu.make_async_remote_copy(
                src_ref=x_ref.at[:, pl.ds(pl.multiple_of(peer * width, width), width)],
                dst_ref=cols_ref.at[mine, :],
                send_sem=send_sem.at[step],
                recv_sem=recv_sem.at[step],
                device_id={"tensor": peer},
                device_id_type=MESH,
            )
        )
    for copy in copies:
        copy.start()
    own = pltpu.make_async_copy(
        x_ref.at[:, pl.ds(pl.multiple_of(me * width, width), width)],
        cols_ref.at[mine, :],
        send_sem.at[0],
    )
    own.start()
    attend(q_ref, g_ref, k_ref, v_ref, bias_ref, cos_ref, sin_ref, out_ref)
    own.wait()
    for copy in copies:
        copy.wait()


def attention(n, q, g, k, v, bias, cosine, sine, x):
    tokens, width = q.shape
    vmem = pl.BlockSpec(memory_space=pltpu.VMEM)
    return pl.pallas_call(
        functools.partial(attention_kernel, n),
        out_shape=(
            jax.ShapeDtypeStruct((tokens, width), bf16),
            jax.ShapeDtypeStruct((tokens, x.shape[1] // n), bf16),
        ),
        in_specs=[vmem] * 8,
        out_specs=(vmem, vmem),
        scratch_shapes=[pltpu.SemaphoreType.DMA((n,)), pltpu.SemaphoreType.DMA((n,))],
        compiler_params=pltpu.CompilerParams(
            collective_id=0, has_side_effects=True, vmem_limit_bytes=40 * 2**20
        ),
        cost_estimate=pl.CostEstimate(
            flops=8 * tokens * tokens * width, bytes_accessed=8 * tokens * width,
            transcendentals=tokens * tokens * width // HD,
        ),
    )(q, g, k, v, bias, cosine, sine, x)


BLOCK = 64


def hdot(a, b, dims):
    return lax.dot_general(a, b, (dims, ((), ())), precision=highest, preferred_element_type=f32)


def diagonal_inverse(block):
    size = block.shape[0]
    rows = lax.broadcasted_iota(jnp.int32, (size, size), 0)
    lanes = lax.broadcasted_iota(jnp.int32, (size, size), 1)
    wide = jnp.concatenate([block, (rows == lanes).astype(f32)], axis=1)
    row_ids = lax.broadcasted_iota(jnp.int32, (size, 1), 0)
    for k in range(size - 1):
        factor = wide[:, k : k + 1] * (1.0 / wide[k : k + 1, k : k + 1])
        wide = wide - jnp.where(row_ids > k, factor, 0.0) * wide[k : k + 1, :]
    diagonal = jnp.sum(jnp.where(rows == lanes, wide[:, :size], 0.0), axis=1, keepdims=True)
    return wide[:, size:] * lax.rsqrt(diagonal)


def factor_inverse(gram_ref, inv_ref):
    rank = gram_ref.shape[0]
    rows = lax.broadcasted_iota(jnp.int32, (rank, rank), 0)
    lanes = lax.broadcasted_iota(jnp.int32, (rank, rank), 1)
    inv_ref[...] = (rows == lanes).astype(f32)
    for start in range(0, rank, BLOCK):
        end = start + BLOCK
        inner = diagonal_inverse(gram_ref[start:end, start:end])
        top = hdot(inner, inv_ref[start:end, :], ((1,), (0,)))
        inv_ref[start:end, :] = top
        if end < rank:
            panel = hdot(gram_ref[end:, start:end], inner, ((1,), (1,)))
            gram_ref[end:, end:] = gram_ref[end:, end:] - hdot(panel, panel, ((1,), (1,)))
            inv_ref[end:, :] = inv_ref[end:, :] - hdot(panel, top, ((1,), (0,)))


def finish_kernel(proj_ref, mixed_ref, raw_ref, grad_ref, left_ref, right_ref, gram, inv):
    gram[...] = hdot(proj_ref[...], mixed_ref[...], ((0,), (0,)))
    factor_inverse(gram, inv)
    left_ref[...] = hdot(raw_ref[...], inv[...], ((1,), (1,))) * math.sqrt(D)
    orth = hdot(mixed_ref[...], inv[...], ((1,), (1,)))
    high = orth.astype(bf16)
    low = (orth - high.astype(f32)).astype(bf16)
    grad = grad_ref[...]
    dims = (((0,), (0,)), ((), ()))
    right_ref[...] = lax.dot_general(
        grad, high, dims, preferred_element_type=f32
    ) + lax.dot_general(grad, low, dims, preferred_element_type=f32)


def finish(projected, mixed, raw, grad):
    rank = projected.shape[1]
    vmem = pl.BlockSpec(memory_space=pltpu.VMEM)
    return pl.pallas_call(
        finish_kernel,
        out_shape=(
            jax.ShapeDtypeStruct(raw.shape, f32),
            jax.ShapeDtypeStruct((grad.shape[1], rank), f32),
        ),
        in_specs=[vmem] * 4,
        out_specs=(vmem, vmem),
        scratch_shapes=[pltpu.VMEM((rank, rank), f32), pltpu.VMEM((rank, rank), f32)],
        compiler_params=pltpu.CompilerParams(vmem_limit_bytes=40 * 2**20),
        cost_estimate=pl.CostEstimate(flops=10**10, bytes_accessed=10**7, transcendentals=0),
    )(projected, mixed, raw, grad)


def pieces(wide, count=3):
    out = []
    for _ in range(count):
        out.append(wide.astype(bf16))
        wide = wide - out[-1].astype(f32)
    return out


def exact_dot(low, wide, dims, count=3):
    return sum(
        lax.dot_general(low, piece, (dims, ((), ())), preferred_element_type=f32)
        for piece in pieces(wide, count)
    )


def local(queries, key_rows, value_rows, out_grad, layer_input, query_weight, dion_basis, lengths):
    token_count = queries.shape[1]
    local_heads = queries.shape[2] // HD
    tensor_count = lax.axis_size("tensor")
    tensor_index = lax.axis_index("tensor")
    bias, cosine, sine = tree_layout(lengths[0], token_count)
    group_head = tensor_index * local_heads // GROUP
    key_block = lax.dynamic_slice_in_dim(key_rows[0], group_head * HD, HD, 1)
    value_block = lax.dynamic_slice_in_dim(value_rows[0], group_head * HD, HD, 1)
    query_grad, columns = attention(
        tensor_count, queries[0], out_grad[0], key_block, value_block, bias, cosine, sine,
        layer_input[0],
    )
    projected = lax.psum(exact_dot(query_grad, dion_basis[0], ((1,), (0,))), "tensor")
    layer_grad = lax.psum_scatter(
        nt(query_grad, query_weight[0]).astype(bf16), "tensor", scatter_dimension=0, tiled=True
    )
    upstream = shifted(layer_grad, "section", -1)
    left_raw = exact_dot(columns, projected, ((0,), (0,)))
    mixed = lax.psum(exact_dot(columns, left_raw, ((1,), (0,))), "tensor")
    left_factor, right_factor = finish(projected, mixed, left_raw, query_grad)
    return (upstream[None], left_factor[None], right_factor[None])


def solution(mesh):
    placed = (
        P("section", None, "tensor"),
        P("section", None, None),
        P("section", None, None),
        P("section", None, "tensor"),
        P("section", "tensor", None),
        P("section", None, "tensor"),
        P("section", "tensor", None),
        P("section", None),
    )
    return jax.shard_map(
        local,
        mesh=mesh,
        in_specs=placed,
        out_specs=(
            P("section", "tensor", None),
            P("section", "tensor", None),
            P("section", "tensor", None),
        ),
        check_vma=False,
    )
```

```python
import functools
import math

import jax
import jax.numpy as jnp
from jax import lax
from jax.experimental import pallas as pl
from jax.experimental.pallas import tpu as pltpu
from jax.sharding import PartitionSpec as P

D = 8192
HD = 128
GROUP = 8
MESH = pl.DeviceIdType.MESH

rope_base = 500000.0
highest = lax.Precision.HIGHEST
f32 = jnp.float32
bf16 = jnp.bfloat16


def tree_layout(lengths_row, token_count):
    token_ids = jnp.arange(token_count, dtype=jnp.int32)
    bound_one = lengths_row[0]
    bound_two = lengths_row[0] + lengths_row[1]
    positions = jnp.where(token_ids < bound_two, token_ids, token_ids - lengths_row[1]).astype(f32)
    row_ids = token_ids[:, None]
    col_ids = token_ids[None, :]
    crossed = (row_ids >= bound_two) & (col_ids >= bound_one) & (col_ids < bound_two)
    visible = (col_ids <= row_ids) & jnp.logical_not(crossed)
    bias = jnp.where(visible, 0.0, -1e30).astype(f32)
    freq_ids = jnp.arange(HD // 2, dtype=f32)
    inverse = jnp.exp(-math.log(rope_base) * 2.0 * freq_ids / HD)
    angles = positions[:, None] * inverse[None, :]
    scale = 1.0 / math.sqrt(HD)
    cosine, sine = jnp.cos(angles) * scale, jnp.sin(angles) * scale
    return (
        bias,
        jnp.concatenate([cosine, cosine], axis=-1),
        jnp.concatenate([sine, -sine], axis=-1),
    )


def nt(a, b):
    return lax.dot_general(a, b, (((1,), (1,)), ((), ())), preferred_element_type=f32)


def attend(q_ref, g_ref, k_ref, v_ref, bias_ref, cos_ref, sin_ref, out_ref):
    tokens, width = q_ref.shape
    half = tokens // 2
    scale = 1.0 / math.sqrt(HD)

    def head(h, carry):
        lanes = pl.ds(pl.multiple_of(h * HD, HD), HD)
        for part in range(2):
            rows, seen = pl.ds(part * half, half), pl.ds(0, (part + 1) * half)
            keys, values = k_ref[seen, :], v_ref[seen, :]
            q, g = q_ref[rows, lanes], g_ref[rows, lanes]
            scores = nt(q, keys) * scale + bias_ref[rows, seen]
            exps = jnp.exp(scores - jnp.max(scores, axis=-1, keepdims=True))
            weights = exps * (1.0 / jnp.sum(exps, axis=-1, keepdims=True))
            outputs = jnp.dot(weights.astype(bf16), values, preferred_element_type=f32)
            out_dot = jnp.sum(g.astype(f32) * outputs, axis=-1, keepdims=True)
            score_grad = (weights * (nt(g, values) - out_dot)).astype(bf16)
            rotated = jnp.dot(score_grad, keys, preferred_element_type=f32)
            swapped = jnp.concatenate([rotated[:, HD // 2 :], rotated[:, : HD // 2]], axis=-1)
            out_ref[rows, lanes] = (
                rotated * cos_ref[rows, :] + swapped * sin_ref[rows, :]
            ).astype(bf16)
        return carry

    lax.fori_loop(0, width // HD, head, 0)


def attention_kernel(
    n, q_ref, g_ref, k_ref, v_ref, bias_ref, cos_ref, sin_ref, x_ref, out_ref, cols_ref,
    send_sem, recv_sem,
):
    me = lax.axis_index("tensor")
    rows = x_ref.shape[0]
    width = x_ref.shape[1] // n
    barrier = pltpu.get_barrier_semaphore()
    for step in range(1, n):
        pl.semaphore_signal(
            barrier, inc=1, device_id={"tensor": lax.rem(me + step, n)}, device_id_type=MESH
        )
    pl.semaphore_wait(barrier, n - 1)
    mine = pl.ds(pl.multiple_of(me * rows, rows), rows)
    copies = []
    for step in range(1, n):
        peer = lax.rem(me + step, n)
        copies.append(
            pltpu.make_async_remote_copy(
                src_ref=x_ref.at[:, pl.ds(pl.multiple_of(peer * width, width), width)],
                dst_ref=cols_ref.at[mine, :],
                send_sem=send_sem.at[step],
                recv_sem=recv_sem.at[step],
                device_id={"tensor": peer},
                device_id_type=MESH,
            )
        )
    for copy in copies:
        copy.start()
    own = pltpu.make_async_copy(
        x_ref.at[:, pl.ds(pl.multiple_of(me * width, width), width)],
        cols_ref.at[mine, :],
        send_sem.at[0],
    )
    own.start()
    attend(q_ref, g_ref, k_ref, v_ref, bias_ref, cos_ref, sin_ref, out_ref)
    own.wait()
    for copy in copies:
        copy.wait()


def attention(n, q, g, k, v, bias, cosine, sine, x):
    tokens, width = q.shape
    vmem = pl.BlockSpec(memory_space=pltpu.VMEM)
    return pl.pallas_call(
        functools.partial(attention_kernel, n),
        out_shape=(
            jax.ShapeDtypeStruct((tokens, width), bf16),
            jax.ShapeDtypeStruct((tokens, x.shape[1] // n), bf16),
        ),
        in_specs=[vmem] * 8,
        out_specs=(vmem, vmem),
        scratch_shapes=[pltpu.SemaphoreType.DMA((n,)), pltpu.SemaphoreType.DMA((n,))],
        compiler_params=pltpu.CompilerParams(
            collective_id=0, has_side_effects=True, vmem_limit_bytes=40 * 2**20
        ),
        cost_estimate=pl.CostEstimate(
            flops=8 * tokens * tokens * width, bytes_accessed=8 * tokens * width,
            transcendentals=tokens * tokens * width // HD,
        ),
    )(q, g, k, v, bias, cosine, sine, x)


BLOCK = 64


def hdot(a, b, dims):
    return lax.dot_general(a, b, (dims, ((), ())), precision=highest, preferred_element_type=f32)


def diagonal_inverse(block):
    size = block.shape[0]
    rows = lax.broadcasted_iota(jnp.int32, (size, size), 0)
    lanes = lax.broadcasted_iota(jnp.int32, (size, size), 1)
    wide = jnp.concatenate([block, (rows == lanes).astype(f32)], axis=1)
    row_ids = lax.broadcasted_iota(jnp.int32, (size, 1), 0)
    for k in range(size - 1):
        factor = wide[:, k : k + 1] * (1.0 / wide[k : k + 1, k : k + 1])
        wide = wide - jnp.where(row_ids > k, factor, 0.0) * wide[k : k + 1, :]
    diagonal = jnp.sum(jnp.where(rows == lanes, wide[:, :size], 0.0), axis=1, keepdims=True)
    return wide[:, size:] * lax.rsqrt(diagonal)


def factor_inverse(gram_ref, inv_ref, between):
    rank = gram_ref.shape[0]
    rows = lax.broadcasted_iota(jnp.int32, (rank, rank), 0)
    lanes = lax.broadcasted_iota(jnp.int32, (rank, rank), 1)
    inv_ref[...] = (rows == lanes).astype(f32)
    for start in range(0, rank, BLOCK):
        end = start + BLOCK
        inner = diagonal_inverse(gram_ref[start:end, start:end])
        top = hdot(inner, inv_ref[start:end, :], ((1,), (0,)))
        inv_ref[start:end, :] = top
        if end < rank:
            panel = hdot(gram_ref[end:, start:end], inner, ((1,), (1,)))
            gram_ref[end:, end:] = gram_ref[end:, end:] - hdot(panel, panel, ((1,), (1,)))
            inv_ref[end:, :] = inv_ref[end:, :] - hdot(panel, top, ((1,), (0,)))
        between(end // BLOCK)


def pieces(wide, count=3):
    out = []
    for _ in range(count):
        out.append(wide.astype(bf16))
        wide = wide - out[-1].astype(f32)
    return out


def exact_dot(low, wide, dims, count=3):
    return sum(
        lax.dot_general(low, piece, (dims, ((), ())), preferred_element_type=f32)
        for piece in pieces(wide, count)
    )


CHUNKS = 8


def dion_kernel(
    n, sections, grad_ref, weight_ref, cols_ref, basis_ref, up_ref, left_ref, right_ref,
    wbuf, part, sib, from_left, from_right, gram, inv, raw,
    p_part, p_sib, p_recv, p_full, m_part, m_sib, m_recv, m_full,
    w_sem, pair_sem, right_sem, left_sem, shift_sem, p_sem, m_sem,
):
    chips = n // 2
    me = lax.axis_index("tensor")
    section = lax.axis_index("section")
    chip, core = me // 2, lax.rem(me, 2)
    other = 1 - core
    tokens = grad_ref.shape[0]
    rows = tokens // n
    rank = basis_ref.shape[1]
    chunk = wbuf.shape[1]
    sibling = {"tensor": chip * 2 + other}
    first, last = section == 0, section == sections - 1

    def load(j):
        return pltpu.make_async_copy(
            weight_ref.at[pl.ds(j * chunk, chunk), :], wbuf.at[j], w_sem.at[j]
        )

    for j in range(CHUNKS):
        load(j).start()

    def remote(src, dst, sems, index, device):
        return pltpu.make_async_remote_copy(
            src_ref=src, dst_ref=dst, send_sem=sems.at[(0, *index)], recv_sem=sems.at[(1, *index)],
            device_id=device, device_id_type=MESH,
        )

    barrier = pltpu.get_barrier_semaphore()

    def greet(device):
        pl.semaphore_signal(barrier, inc=1, device_id=device, device_id_type=MESH)

    greet(sibling)
    for step in range(1, chips):
        greet({"tensor": lax.rem(chip + step, chips) * 2 + core})

    greet({"section": lax.rem(section + sections - 1, sections)})
    greet({"section": lax.rem(section + 1, sections)})
    pl.semaphore_wait(barrier, chips + 2)

    class Reduce:
        def __init__(self, part, sib, recv, full, sems):
            self.part, self.sib, self.recv, self.full, self.sems = part, sib, recv, full, sems

        def one(self):
            return remote(self.part.at[:, other], self.sib, self.sems, (0,), sibling)

        def two(self, step):
            peer = lax.rem(chip + step, chips)
            return remote(
                self.part.at[peer, core], self.recv.at[step], self.sems, (step,),
                {"tensor": peer * 2 + core},
            )

        def three(self, step):
            peer = lax.rem(chip + step, chips)
            slot = self.full.at[chip, core]
            return remote(slot, slot, self.sems, (chips + step,), {"tensor": peer * 2 + core})

        def four(self):
            slot = self.full.at[:, core]
            return remote(slot, slot, self.sems, (chips,), sibling)

        def start(self, value):
            self.part[...] = value.reshape(chips, 2, rows, rank)
            self.one().start()

        def scatter(self):
            self.one().wait_recv()
            self.part[:, core] = self.part[:, core] + self.sib[...]
            for step in range(1, chips):
                self.two(step).start()

        def gather(self):
            total = self.part[chip, core]
            for step in range(1, chips):
                self.two(step).wait_recv()
                total = total + self.recv[step]
            self.full[chip, core] = total
            for step in range(1, chips):
                self.three(step).start()

        def pair(self):
            for step in range(1, chips):
                self.three(step).wait_recv()
            self.four().start()

        def result(self):
            self.four().wait()
            self.one().wait_send()
            for step in range(1, chips):
                self.two(step).wait_send()
                self.three(step).wait_send()
            return self.full[...].reshape(tokens, rank)

    def send_pair(j):
        return remote(part.at[j, :, other], sib.at[j], pair_sem, (j,), sibling)

    def send_right(j, b):
        return remote(
            part.at[j, b, core], from_left.at[j, b], right_sem, (j, b),
            {"tensor": lax.rem(chip + 1, chips) * 2 + core},
        )

    def send_left(j, b):
        return remote(
            part.at[j, b, core], from_right.at[j, b], left_sem, (j, b),
            {"tensor": lax.rem(chip + chips - 1, chips) * 2 + core},
        )

    def send_shift(j):
        return remote(
            part.at[j, chip, core], up_ref.at[:, pl.ds(j * chunk, chunk)], shift_sem, (j,),
            {"section": lax.rem(section + sections - 1, sections)},
        )

    def multiply(j):
        load(j).wait()

        def tile(t, carry):
            lanes = pl.ds(pl.multiple_of(t * 256, 256), 256)
            out = nt(grad_ref[...], wbuf[j, lanes, :]).astype(bf16)
            part[j, :, :, :, lanes] = out.reshape(chips, 2, rows, 256)
            return carry

        lax.fori_loop(0, chunk // 256, tile, 0)
        send_pair(j).start()

    def pair_sum(j):
        send_pair(j).wait_recv()
        part[j, :, core] = (part[j, :, core].astype(f32) + sib[j].astype(f32)).astype(bf16)

        @pl.when(chip == 0)
        def _():
            for b in range(chips - 1, 0, -1):
                send_right(j, b).start()

        @pl.when(chip == chips - 1)
        def _():
            for b in range(chips - 1):
                send_left(j, b).start()

    def add_to(j, b, arrived):
        part[j, b, core] = (
            part[j, b, core].astype(f32) + arrived[j, b].astype(f32)
        ).astype(bf16)

    def hop(j):
        for b in range(chips - 1, 0, -1):

            @pl.when((chip > 0) & (chip < b))
            def _():
                send_right(j, b).wait_recv()
                add_to(j, b, from_left)
                send_right(j, b).start()

        for b in range(chips - 1):

            @pl.when((chip < chips - 1) & (chip > b))
            def _():
                send_left(j, b).wait_recv()
                add_to(j, b, from_right)
                send_left(j, b).start()

        for b in range(chips):

            @pl.when(chip == b)
            def _():
                if b > 0:
                    send_right(j, b).wait_recv()
                    add_to(j, b, from_left)
                if b < chips - 1:
                    send_left(j, b).wait_recv()
                    add_to(j, b, from_right)

        @pl.when(jnp.logical_not(first))
        def _():
            send_shift(j).start()

    projected_sum = Reduce(p_part, p_sib, p_recv, p_full, p_sem)
    mixed_sum = Reduce(m_part, m_sib, m_recv, m_full, m_sem)
    projected_sum.start(exact_dot(grad_ref[...], basis_ref[...], ((1,), (0,))))
    multiply(0)
    projected_sum.scatter()
    multiply(1)
    pair_sum(0)
    projected_sum.gather()
    multiply(2)
    pair_sum(1)
    projected_sum.pair()
    multiply(3)
    pair_sum(2)
    projected = projected_sum.result()
    raw[...] = exact_dot(cols_ref[...], projected, ((0,), (0,)))
    mixed_sum.start(exact_dot(cols_ref[...], raw[...], ((1,), (0,))))
    multiply(4)
    pair_sum(3)
    mixed_sum.scatter()
    multiply(5)
    pair_sum(4)
    mixed_sum.gather()
    multiply(6)
    pair_sum(5)
    mixed_sum.pair()
    multiply(7)
    pair_sum(6)
    pair_sum(7)
    hop(0)
    mixed = mixed_sum.result()
    gram[...] = hdot(p_full[...].reshape(tokens, rank), mixed, ((0,), (0,)))
    factor_inverse(gram, inv, hop)
    left_ref[...] = hdot(raw[...], inv[...], ((1,), (1,))) * math.sqrt(D)
    orth = hdot(m_full[...].reshape(tokens, rank), inv[...], ((1,), (1,)))
    right_ref[...] = exact_dot(grad_ref[...], orth, ((0,), (0,)), 2)
    for j in range(rank // BLOCK + 1, CHUNKS):
        hop(j)

    @pl.when(last)
    def _():
        up_ref[...] = jnp.zeros_like(up_ref)

    for j in range(CHUNKS):

        @pl.when(jnp.logical_not(last))
        def _():
            send_shift(j).wait_recv()

        @pl.when(jnp.logical_not(first))
        def _():
            send_shift(j).wait_send()

        send_pair(j).wait_send()
        for b in range(chips):

            @pl.when(chip < b)
            def _():
                send_right(j, b).wait_send()

            @pl.when(chip > b)
            def _():
                send_left(j, b).wait_send()


def dion(n, sections, grad, weight, columns, basis):
    tokens, width = grad.shape
    rank = basis.shape[1]
    chips, rows = n // 2, tokens // n
    depth = weight.shape[0]
    chunk = depth // CHUNKS
    vmem = pl.BlockSpec(memory_space=pltpu.VMEM)
    reduce_scratch = [
        pltpu.VMEM((chips, 2, rows, rank), f32),
        pltpu.VMEM((chips, rows, rank), f32),
        pltpu.VMEM((chips, rows, rank), f32),
        pltpu.VMEM((chips, 2, rows, rank), f32),
    ]
    dma = pltpu.SemaphoreType.DMA
    return pl.pallas_call(
        functools.partial(dion_kernel, n, sections),
        out_shape=(
            jax.ShapeDtypeStruct((rows, depth), bf16),
            jax.ShapeDtypeStruct((columns.shape[1], rank), f32),
            jax.ShapeDtypeStruct((width, rank), f32),
        ),
        in_specs=[vmem, pl.BlockSpec(memory_space=pl.ANY), vmem, vmem],
        out_specs=(vmem, vmem, vmem),
        scratch_shapes=[
            pltpu.VMEM((CHUNKS, chunk, width), bf16),
            pltpu.VMEM((CHUNKS, chips, 2, rows, chunk), bf16),
            pltpu.VMEM((CHUNKS, chips, rows, chunk), bf16),
            pltpu.VMEM((CHUNKS, chips, rows, chunk), bf16),
            pltpu.VMEM((CHUNKS, chips, rows, chunk), bf16),
            pltpu.VMEM((rank, rank), f32),
            pltpu.VMEM((rank, rank), f32),
            pltpu.VMEM((columns.shape[1], rank), f32),
            *reduce_scratch,
            *reduce_scratch,
            dma((CHUNKS,)),
            dma((2, CHUNKS)),
            dma((2, CHUNKS, chips)),
            dma((2, CHUNKS, chips)),
            dma((2, CHUNKS)),
            dma((2, 2 * chips)),
            dma((2, 2 * chips)),
        ],
        compiler_params=pltpu.CompilerParams(
            collective_id=1, has_side_effects=True, vmem_limit_bytes=60 * 2**20
        ),
        cost_estimate=pl.CostEstimate(
            flops=2 * tokens * width * depth, bytes_accessed=2 * width * depth, transcendentals=0
        ),
    )(grad, weight, columns, basis)


def local(queries, key_rows, value_rows, out_grad, layer_input, query_weight, dion_basis, lengths):
    token_count = queries.shape[1]
    local_heads = queries.shape[2] // HD
    tensor_count = lax.axis_size("tensor")
    tensor_index = lax.axis_index("tensor")
    bias, cosine, sine = tree_layout(lengths[0], token_count)
    group_head = tensor_index * local_heads // GROUP
    key_block = lax.dynamic_slice_in_dim(key_rows[0], group_head * HD, HD, 1)
    value_block = lax.dynamic_slice_in_dim(value_rows[0], group_head * HD, HD, 1)
    query_grad, columns = attention(
        tensor_count, queries[0], out_grad[0], key_block, value_block, bias, cosine, sine,
        layer_input[0],
    )
    upstream, left_factor, right_factor = dion(
        tensor_count, lax.axis_size("section"), query_grad, query_weight[0], columns, dion_basis[0]
    )
    return (upstream[None], left_factor[None], right_factor[None])


def solution(mesh):
    placed = (
        P("section", None, "tensor"),
        P("section", None, None),
        P("section", None, None),
        P("section", None, "tensor"),
        P("section", "tensor", None),
        P("section", None, "tensor"),
        P("section", "tensor", None),
        P("section", None),
    )
    return jax.shard_map(
        local,
        mesh=mesh,
        in_specs=placed,
        out_specs=(
            P("section", "tensor", None),
            P("section", "tensor", None),
            P("section", "tensor", None),
        ),
        check_vma=False,
    )
```

```python
import functools
import math

import jax
import jax.numpy as jnp
from jax import lax
from jax.experimental import pallas as pl
from jax.experimental.pallas import tpu as pltpu
from jax.sharding import PartitionSpec as P

D = 8192
HD = 128
GROUP = 8
MESH = pl.DeviceIdType.MESH

rope_base = 500000.0
highest = lax.Precision.HIGHEST
f32 = jnp.float32
bf16 = jnp.bfloat16


def tree_layout(lengths_row, token_count):
    token_ids = jnp.arange(token_count, dtype=jnp.int32)
    bound_one = lengths_row[0]
    bound_two = lengths_row[0] + lengths_row[1]
    positions = jnp.where(token_ids < bound_two, token_ids, token_ids - lengths_row[1]).astype(f32)
    row_ids = token_ids[:, None]
    col_ids = token_ids[None, :]
    crossed = (row_ids >= bound_two) & (col_ids >= bound_one) & (col_ids < bound_two)
    visible = (col_ids <= row_ids) & jnp.logical_not(crossed)
    bias = jnp.where(visible, 0.0, -1e30).astype(f32)
    freq_ids = jnp.arange(HD // 2, dtype=f32)
    inverse = jnp.exp(-math.log(rope_base) * 2.0 * freq_ids / HD)
    angles = positions[:, None] * inverse[None, :]
    scale = 1.0 / math.sqrt(HD)
    cosine, sine = jnp.cos(angles) * scale, jnp.sin(angles) * scale
    return (
        bias,
        jnp.concatenate([cosine, cosine], axis=-1),
        jnp.concatenate([sine, -sine], axis=-1),
    )


def nt(a, b):
    return lax.dot_general(a, b, (((1,), (1,)), ((), ())), preferred_element_type=f32)


def attend(q_ref, g_ref, k_ref, v_ref, bias_ref, cos_ref, sin_ref, out_ref):
    tokens, width = q_ref.shape
    half = tokens // 2
    scale = 1.0 / math.sqrt(HD)

    def head(h, carry):
        lanes = pl.ds(pl.multiple_of(h * HD, HD), HD)
        for part in range(2):
            rows, seen = pl.ds(part * half, half), pl.ds(0, (part + 1) * half)
            keys, values = k_ref[seen, :], v_ref[seen, :]
            q, g = q_ref[rows, lanes], g_ref[rows, lanes]
            scores = nt(q, keys) * scale + bias_ref[rows, seen]
            exps = jnp.exp(scores - jnp.max(scores, axis=-1, keepdims=True))
            weights = exps * (1.0 / jnp.sum(exps, axis=-1, keepdims=True))
            outputs = jnp.dot(weights.astype(bf16), values, preferred_element_type=f32)
            out_dot = jnp.sum(g.astype(f32) * outputs, axis=-1, keepdims=True)
            score_grad = (weights * (nt(g, values) - out_dot)).astype(bf16)
            rotated = jnp.dot(score_grad, keys, preferred_element_type=f32)
            swapped = jnp.concatenate([rotated[:, HD // 2 :], rotated[:, : HD // 2]], axis=-1)
            out_ref[rows, lanes] = (
                rotated * cos_ref[rows, :] + swapped * sin_ref[rows, :]
            ).astype(bf16)
        return carry

    lax.fori_loop(0, width // HD, head, 0)


def attention_kernel(
    n, q_ref, g_ref, k_ref, v_ref, bias_ref, cos_ref, sin_ref, x_ref, out_ref, cols_ref,
    send_sem, recv_sem,
):
    me = lax.axis_index("tensor")
    rows = x_ref.shape[0]
    width = x_ref.shape[1] // n
    barrier = pltpu.get_barrier_semaphore()
    for step in range(1, n):
        pl.semaphore_signal(
            barrier, inc=1, device_id={"tensor": lax.rem(me + step, n)}, device_id_type=MESH
        )
    pl.semaphore_wait(barrier, n - 1)
    mine = pl.ds(pl.multiple_of(me * rows, rows), rows)
    copies = []
    for step in range(1, n):
        peer = lax.rem(me + step, n)
        copies.append(
            pltpu.make_async_remote_copy(
                src_ref=x_ref.at[:, pl.ds(pl.multiple_of(peer * width, width), width)],
                dst_ref=cols_ref.at[mine, :],
                send_sem=send_sem.at[step],
                recv_sem=recv_sem.at[step],
                device_id={"tensor": peer},
                device_id_type=MESH,
            )
        )
    for copy in copies:
        copy.start()
    own = pltpu.make_async_copy(
        x_ref.at[:, pl.ds(pl.multiple_of(me * width, width), width)],
        cols_ref.at[mine, :],
        send_sem.at[0],
    )
    own.start()
    attend(q_ref, g_ref, k_ref, v_ref, bias_ref, cos_ref, sin_ref, out_ref)
    own.wait()
    for copy in copies:
        copy.wait()


def attention(n, q, g, k, v, bias, cosine, sine, x):
    tokens, width = q.shape
    vmem = pl.BlockSpec(memory_space=pltpu.VMEM)
    return pl.pallas_call(
        functools.partial(attention_kernel, n),
        out_shape=(
            jax.ShapeDtypeStruct((tokens, width), bf16),
            jax.ShapeDtypeStruct((tokens, x.shape[1] // n), bf16),
        ),
        in_specs=[vmem] * 8,
        out_specs=(vmem, vmem),
        scratch_shapes=[pltpu.SemaphoreType.DMA((n,)), pltpu.SemaphoreType.DMA((n,))],
        compiler_params=pltpu.CompilerParams(
            collective_id=0, has_side_effects=True, vmem_limit_bytes=40 * 2**20
        ),
        cost_estimate=pl.CostEstimate(
            flops=8 * tokens * tokens * width, bytes_accessed=8 * tokens * width,
            transcendentals=tokens * tokens * width // HD,
        ),
    )(q, g, k, v, bias, cosine, sine, x)


BLOCK = 64


def hdot(a, b, dims):
    return lax.dot_general(a, b, (dims, ((), ())), precision=highest, preferred_element_type=f32)


def diagonal_inverse(block):
    size = block.shape[0]
    rows = lax.broadcasted_iota(jnp.int32, (size, size), 0)
    lanes = lax.broadcasted_iota(jnp.int32, (size, size), 1)
    wide = jnp.concatenate([block, (rows == lanes).astype(f32)], axis=1)
    row_ids = lax.broadcasted_iota(jnp.int32, (size, 1), 0)
    for k in range(size - 1):
        factor = wide[:, k : k + 1] * (1.0 / wide[k : k + 1, k : k + 1])
        wide = wide - jnp.where(row_ids > k, factor, 0.0) * wide[k : k + 1, :]
    diagonal = jnp.sum(jnp.where(rows == lanes, wide[:, :size], 0.0), axis=1, keepdims=True)
    return wide[:, size:] * lax.rsqrt(diagonal)


def factor_inverse(gram_ref, inv_ref, between):
    rank = gram_ref.shape[0]
    rows = lax.broadcasted_iota(jnp.int32, (rank, rank), 0)
    lanes = lax.broadcasted_iota(jnp.int32, (rank, rank), 1)
    inv_ref[...] = (rows == lanes).astype(f32)
    for start in range(0, rank, BLOCK):
        end = start + BLOCK
        inner = diagonal_inverse(gram_ref[start:end, start:end])
        top = hdot(inner, inv_ref[start:end, :], ((1,), (0,)))
        inv_ref[start:end, :] = top
        if end < rank:
            panel = hdot(gram_ref[end:, start:end], inner, ((1,), (1,)))
            gram_ref[end:, end:] = gram_ref[end:, end:] - hdot(panel, panel, ((1,), (1,)))
            inv_ref[end:, :] = inv_ref[end:, :] - hdot(panel, top, ((1,), (0,)))
        between(end // BLOCK)


def pieces(wide, count=3):
    out = []
    for _ in range(count):
        out.append(wide.astype(bf16))
        wide = wide - out[-1].astype(f32)
    return out


def exact_dot(low, wide, dims, count=3):
    return sum(
        lax.dot_general(low, piece, (dims, ((), ())), preferred_element_type=f32)
        for piece in pieces(wide, count)
    )


CHUNKS = 8


def dion_kernel(
    n, sections, grad_ref, weight_ref, cols_ref, basis_ref, up_ref, left_ref, right_ref,
    wbuf, part, sib, from_left, from_right, gram, inv, raw,
    p_part, p_sib, p_recv, p_full, m_part, m_sib, m_recv, m_full,
    w_sem, pair_sem, right_sem, left_sem, shift_sem, p_sem, m_sem,
):
    chips = n // 2
    me = lax.axis_index("tensor")
    section = lax.axis_index("section")
    chip, core = me // 2, lax.rem(me, 2)
    other = 1 - core
    tokens = grad_ref.shape[0]
    rows = tokens // n
    rank = basis_ref.shape[1]
    chunk = wbuf.shape[1]
    sibling = {"tensor": chip * 2 + other}
    first, last = section == 0, section == sections - 1

    def load(j):
        return pltpu.make_async_copy(
            weight_ref.at[pl.ds(j * chunk, chunk), :], wbuf.at[j], w_sem.at[j]
        )

    for j in range(CHUNKS):
        load(j).start()

    def remote(src, dst, sems, index, device):
        return pltpu.make_async_remote_copy(
            src_ref=src, dst_ref=dst, send_sem=sems.at[(0, *index)], recv_sem=sems.at[(1, *index)],
            device_id=device, device_id_type=MESH,
        )

    barrier = pltpu.get_barrier_semaphore()

    def greet(device):
        pl.semaphore_signal(barrier, inc=1, device_id=device, device_id_type=MESH)

    greet(sibling)
    for step in range(1, chips):
        greet({"tensor": lax.rem(chip + step, chips) * 2 + core})

    greet({"section": lax.rem(section + sections - 1, sections)})
    greet({"section": lax.rem(section + 1, sections)})
    pl.semaphore_wait(barrier, chips + 2)

    class Reduce:
        def __init__(self, part, sib, recv, full, sems):
            self.part, self.sib, self.recv, self.full, self.sems = part, sib, recv, full, sems

        def one(self):
            return remote(self.part.at[:, other], self.sib, self.sems, (0,), sibling)

        def two(self, step):
            peer = lax.rem(chip + step, chips)
            return remote(
                self.part.at[peer, core], self.recv.at[step], self.sems, (step,),
                {"tensor": peer * 2 + core},
            )

        def three(self, step):
            peer = lax.rem(chip + step, chips)
            slot = self.full.at[chip, core]
            return remote(slot, slot, self.sems, (chips + step,), {"tensor": peer * 2 + core})

        def four(self):
            slot = self.full.at[:, core]
            return remote(slot, slot, self.sems, (chips,), sibling)

        def start(self, value):
            self.part[...] = value.reshape(chips, 2, rows, rank)
            self.one().start()

        def scatter(self):
            self.one().wait_recv()
            self.part[:, core] = self.part[:, core] + self.sib[...]
            for step in range(1, chips):
                self.two(step).start()

        def gather(self):
            total = self.part[chip, core]
            for step in range(1, chips):
                self.two(step).wait_recv()
                total = total + self.recv[step]
            self.full[chip, core] = total
            for step in range(1, chips):
                self.three(step).start()

        def pair(self):
            for step in range(1, chips):
                self.three(step).wait_recv()
            self.four().start()

        def result(self):
            self.four().wait()
            self.one().wait_send()
            for step in range(1, chips):
                self.two(step).wait_send()
                self.three(step).wait_send()
            return self.full[...].reshape(tokens, rank)

    def send_pair(j):
        return remote(part.at[j, :, other], sib.at[j], pair_sem, (j,), sibling)

    def send_right(j, b):
        return remote(
            part.at[j, b, core], from_left.at[j, b], right_sem, (j, b),
            {"tensor": lax.rem(chip + 1, chips) * 2 + core},
        )

    def send_left(j, b):
        return remote(
            part.at[j, b, core], from_right.at[j, b], left_sem, (j, b),
            {"tensor": lax.rem(chip + chips - 1, chips) * 2 + core},
        )

    def send_shift(j):
        return remote(
            part.at[j, chip, core], up_ref.at[:, pl.ds(j * chunk, chunk)], shift_sem, (j,),
            {"section": lax.rem(section + sections - 1, sections)},
        )

    def multiply(j):
        load(j).wait()

        def tile(t, carry):
            lanes = pl.ds(pl.multiple_of(t * 256, 256), 256)
            out = nt(grad_ref[...], wbuf[j, lanes, :]).astype(bf16)
            part[j, :, :, :, lanes] = out.reshape(chips, 2, rows, 256)
            return carry

        lax.fori_loop(0, chunk // 256, tile, 0)
        send_pair(j).start()

    def pair_sum(j):
        send_pair(j).wait_recv()
        part[j, :, core] = (part[j, :, core].astype(f32) + sib[j].astype(f32)).astype(bf16)

    def inject(j):
        @pl.when(chip == 0)
        def _():
            for b in range(chips - 1, 0, -1):
                send_right(j, b).start()

        @pl.when(chip == chips - 1)
        def _():
            for b in range(chips - 1):
                send_left(j, b).start()

    def add_to(j, b, arrived):
        part[j, b, core] = (
            part[j, b, core].astype(f32) + arrived[j, b].astype(f32)
        ).astype(bf16)

    def hop(j):
        for b in range(chips - 1, 0, -1):

            @pl.when((chip > 0) & (chip < b))
            def _():
                send_right(j, b).wait_recv()
                add_to(j, b, from_left)
                send_right(j, b).start()

        for b in range(chips - 1):

            @pl.when((chip < chips - 1) & (chip > b))
            def _():
                send_left(j, b).wait_recv()
                add_to(j, b, from_right)
                send_left(j, b).start()

        for b in range(chips):

            @pl.when(chip == b)
            def _():
                if b > 0:
                    send_right(j, b).wait_recv()
                    add_to(j, b, from_left)
                if b < chips - 1:
                    send_left(j, b).wait_recv()
                    add_to(j, b, from_right)

        @pl.when(jnp.logical_not(first))
        def _():
            send_shift(j).start()

    projected_sum = Reduce(p_part, p_sib, p_recv, p_full, p_sem)
    mixed_sum = Reduce(m_part, m_sib, m_recv, m_full, m_sem)
    projected_sum.start(exact_dot(grad_ref[...], basis_ref[...], ((1,), (0,))))
    multiply(0)
    projected_sum.scatter()
    multiply(1)
    pair_sum(0)
    projected_sum.gather()
    inject(0)
    multiply(2)
    pair_sum(1)
    projected_sum.pair()
    multiply(3)
    pair_sum(2)
    projected = projected_sum.result()
    raw[...] = exact_dot(cols_ref[...], projected, ((0,), (0,)))
    mixed_sum.start(exact_dot(cols_ref[...], raw[...], ((1,), (0,))))
    multiply(4)
    pair_sum(3)
    mixed_sum.scatter()
    multiply(5)
    pair_sum(4)
    mixed_sum.gather()
    for j in range(1, 5):
        inject(j)
    multiply(6)
    pair_sum(5)
    inject(5)
    mixed_sum.pair()
    multiply(7)
    pair_sum(6)
    inject(6)
    pair_sum(7)
    inject(7)
    hop(0)
    mixed = mixed_sum.result()
    gram[...] = hdot(p_full[...].reshape(tokens, rank), mixed, ((0,), (0,)))
    factor_inverse(gram, inv, hop)
    left_ref[...] = hdot(raw[...], inv[...], ((1,), (1,))) * math.sqrt(D)
    orth = hdot(m_full[...].reshape(tokens, rank), inv[...], ((1,), (1,)))
    right_ref[...] = exact_dot(grad_ref[...], orth, ((0,), (0,)), 2)
    for j in range(rank // BLOCK + 1, CHUNKS):
        hop(j)

    @pl.when(last)
    def _():
        up_ref[...] = jnp.zeros_like(up_ref)

    for j in range(CHUNKS):

        @pl.when(jnp.logical_not(last))
        def _():
            send_shift(j).wait_recv()

        @pl.when(jnp.logical_not(first))
        def _():
            send_shift(j).wait_send()

        send_pair(j).wait_send()
        for b in range(chips):

            @pl.when(chip < b)
            def _():
                send_right(j, b).wait_send()

            @pl.when(chip > b)
            def _():
                send_left(j, b).wait_send()


def dion(n, sections, grad, weight, columns, basis):
    tokens, width = grad.shape
    rank = basis.shape[1]
    chips, rows = n // 2, tokens // n
    depth = weight.shape[0]
    chunk = depth // CHUNKS
    vmem = pl.BlockSpec(memory_space=pltpu.VMEM)
    reduce_scratch = [
        pltpu.VMEM((chips, 2, rows, rank), f32),
        pltpu.VMEM((chips, rows, rank), f32),
        pltpu.VMEM((chips, rows, rank), f32),
        pltpu.VMEM((chips, 2, rows, rank), f32),
    ]
    dma = pltpu.SemaphoreType.DMA
    return pl.pallas_call(
        functools.partial(dion_kernel, n, sections),
        out_shape=(
            jax.ShapeDtypeStruct((rows, depth), bf16),
            jax.ShapeDtypeStruct((columns.shape[1], rank), f32),
            jax.ShapeDtypeStruct((width, rank), f32),
        ),
        in_specs=[vmem, pl.BlockSpec(memory_space=pl.ANY), vmem, vmem],
        out_specs=(vmem, vmem, vmem),
        scratch_shapes=[
            pltpu.VMEM((CHUNKS, chunk, width), bf16),
            pltpu.VMEM((CHUNKS, chips, 2, rows, chunk), bf16),
            pltpu.VMEM((CHUNKS, chips, rows, chunk), bf16),
            pltpu.VMEM((CHUNKS, chips, rows, chunk), bf16),
            pltpu.VMEM((CHUNKS, chips, rows, chunk), bf16),
            pltpu.VMEM((rank, rank), f32),
            pltpu.VMEM((rank, rank), f32),
            pltpu.VMEM((columns.shape[1], rank), f32),
            *reduce_scratch,
            *reduce_scratch,
            dma((CHUNKS,)),
            dma((2, CHUNKS)),
            dma((2, CHUNKS, chips)),
            dma((2, CHUNKS, chips)),
            dma((2, CHUNKS)),
            dma((2, 2 * chips)),
            dma((2, 2 * chips)),
        ],
        compiler_params=pltpu.CompilerParams(
            collective_id=1, has_side_effects=True, vmem_limit_bytes=60 * 2**20
        ),
        cost_estimate=pl.CostEstimate(
            flops=2 * tokens * width * depth, bytes_accessed=2 * width * depth, transcendentals=0
        ),
    )(grad, weight, columns, basis)


def local(queries, key_rows, value_rows, out_grad, layer_input, query_weight, dion_basis, lengths):
    token_count = queries.shape[1]
    local_heads = queries.shape[2] // HD
    tensor_count = lax.axis_size("tensor")
    tensor_index = lax.axis_index("tensor")
    bias, cosine, sine = tree_layout(lengths[0], token_count)
    group_head = tensor_index * local_heads // GROUP
    key_block = lax.dynamic_slice_in_dim(key_rows[0], group_head * HD, HD, 1)
    value_block = lax.dynamic_slice_in_dim(value_rows[0], group_head * HD, HD, 1)
    query_grad, columns = attention(
        tensor_count, queries[0], out_grad[0], key_block, value_block, bias, cosine, sine,
        layer_input[0],
    )
    upstream, left_factor, right_factor = dion(
        tensor_count, lax.axis_size("section"), query_grad, query_weight[0], columns, dion_basis[0]
    )
    return (upstream[None], left_factor[None], right_factor[None])


def solution(mesh):
    placed = (
        P("section", None, "tensor"),
        P("section", None, None),
        P("section", None, None),
        P("section", None, "tensor"),
        P("section", "tensor", None),
        P("section", None, "tensor"),
        P("section", "tensor", None),
        P("section", None),
    )
    return jax.shard_map(
        local,
        mesh=mesh,
        in_specs=placed,
        out_specs=(
            P("section", "tensor", None),
            P("section", "tensor", None),
            P("section", "tensor", None),
        ),
        check_vma=False,
    )
```
